32 devices in a mesh: dom: 2 (over y), grp: 16 (over z, x, core).
Axes of the slice: x: 2, y: 2, z: 4, core: 2. Of those that a mesh axis runs over, the one named last changes fastest.
Arguments:
- routes: int32 [2048, 8], P(('dom', 'grp')), parts along dimension 0, may hold values from 0 to 15, as said below
- gates: float32 [2048, 8], P(('dom', 'grp')), parts along dimension 0, may hold values from 0.05 to 0.6
- hidden: bfloat16 [2048, 8, 1024], P(('dom', 'grp')), parts along dimension 0, may hold values from -6 to 6
- expert_weight: bfloat16 [16, 1024, 3584], P('grp'), may hold values from -0.1875 to 0.1875
- shared_out: bfloat16 [2048, 3584], P(('dom', 'grp')), parts along dimension 0, may hold values from -6 to 6
Outputs:
- combined: bfloat16 [2048, 3584], P(('dom', 'grp')), parts along dimension 0
The draws below stay inside these ranges and needn't reach their ends.
There are 2 independent parts, one for each index of `dom`. The reference program is written for one: setup_inputs(seed, part) draws one part's arguments, and reference() takes and returns one part's arrays. A program takes and returns all parts, laid end to end along the dimension named above; an argument that names none is the same for every part. Nothing has to cross between parts.
Inputs may be any that keep to these rules, and one draw needn't show every extreme that they name: `routes`: each token names 8 different experts, 4 in each of 2 different groups (2 is the smaller of 4 and 2; the group of expert e is e // 8). Among the 64 tokens of one device every group is named by exactly 64 tokens, no expert is named by more than 64 tokens, and one expert exactly 64 times.
All inputs are finite; a program needn't handle non-finite values.
Results may differ from the reference program's by a relative error of at most 0.0065.
Values may be sent and summed in bfloat16 or wider, within the bound.
A program may use at most 64 MiB of HBM per device.

```python
import math
import jax
import jax.numpy as jnp
from jax import lax

D = 3584
FF = 1024
TOK_DEV = 64
TOPK = 8
GROUP_DEV = 8
EXPERTS = 16
GROUPS = 2
TOPG_USED = 2
PER_GROUP = 4
CAP = 64
TOKENS = 1024
N_GRP = 16


def draw_routes(key, part):
    key = jax.random.fold_in(key, 11)

    def one_device(device_key):
        group_key, inner_key = jax.random.split(device_key)
        group_order = jax.random.permutation(group_key, GROUPS)
        inner_keys = jax.random.split(inner_key, GROUPS)
        inner_order = jax.vmap(lambda k: jax.random.permutation(k, GROUP_DEV))(inner_keys)
        token_pos = jnp.arange(TOK_DEV, dtype=jnp.int32)[:, None]
        group_slot = jnp.arange(TOPG_USED, dtype=jnp.int32)[None, :]
        position = token_pos * TOPG_USED + group_slot
        group_rank = position % GROUPS
        user_rank = (position // GROUPS)[:, :, None]
        chosen_group = group_order[group_rank]
        member = jnp.arange(PER_GROUP, dtype=jnp.int32)[None, None, :]
        drawn = (user_rank * PER_GROUP + member) % GROUP_DEV
        first_users = user_rank < CAP
        cycle_index = jnp.where(first_users, user_rank * (PER_GROUP - 1) + member - 1, CAP * (PER_GROUP - 1) + (user_rank - CAP) * PER_GROUP + member)
        others = 1 + cycle_index % (GROUP_DEV - 1)
        heavy = jnp.where(first_users & (member == 0), 0, others)
        local_pick = jnp.where((group_rank == 0)[:, :, None], heavy, drawn)
        expert = chosen_group[:, :, None] * GROUP_DEV + inner_order[chosen_group[:, :, None], local_pick]
        return expert.reshape(TOK_DEV, TOPK).astype(jnp.int32)
    device_keys = jax.vmap(lambda s: jax.random.fold_in(key, s))(jnp.arange(N_GRP, dtype=jnp.int32))
    return jax.vmap(one_device)(device_keys).reshape(TOKENS, TOPK)


def steps_of(rng, extent, cuts, low, high):
    level, own = 1.0, jax.random.fold_in(rng, 6)
    for dim, shards_of in cuts:
        heights = jnp.exp(jax.random.uniform(jax.random.fold_in(own, dim), (shards_of,), jnp.float32, low / len(cuts), high / len(cuts)))
        level = level * jnp.repeat(heights, extent[dim] // shards_of).reshape([-1 if axis == dim else 1 for axis in range(len(extent))])
    return level


def bell_draw(stream_key, extent, width, bound, shards=(), kind=jnp.bfloat16):
    values = width * jax.random.normal(stream_key, extent, jnp.float32)
    if shards:
        values = values * steps_of(stream_key, extent, shards, -0.22, 0.18)
    return jnp.clip(values, -bound, bound).astype(kind)


def setup_inputs(seed: int = 0, part: int = 0) -> dict:
    key_of = jax.random.split(jax.random.key(seed), 6)
    own_keys = jax.random.split(jax.random.fold_in(key_of[5], part), 6)
    routes = draw_routes(jax.random.fold_in(jax.random.fold_in(key_of[5], part), 71), part)
    gates = jnp.clip(jnp.exp(math.log(0.6) - 2.4849067 * jax.random.uniform(own_keys[1], (TOKENS, TOPK), jnp.float32) ** steps_of(own_keys[1], (TOKENS, TOPK), ((0, 16),), -0.2, 0.2)), 0.05, 0.6)
    hidden = bell_draw(own_keys[2], (TOKENS, TOPK, FF), 1.0, 6.0, ((0, 16),))
    expert_weight = bell_draw(key_of[3], (EXPERTS, FF, D), FF ** -0.5, 0.1875, ((0, 16),))
    shared_out = bell_draw(own_keys[4], (TOKENS, D), 1.0, 6.0, ((0, 16),))
    return {"routes": routes, "gates": gates, "hidden": hidden, "expert_weight": expert_weight, "shared_out": shared_out}


def reference(routes, gates, hidden, expert_weight, shared_out):
    per_src = TOK_DEV * TOPK
    expert_ids = routes.reshape(N_GRP, per_src)
    onehot = (expert_ids[:, :, None] == jnp.arange(EXPERTS, dtype=jnp.int32)[None, None, :]).astype(jnp.int32)
    earlier = jnp.cumsum(onehot, axis=1) - onehot
    slot_index = jnp.sum(earlier * onehot, axis=2).astype(jnp.int32)
    sources = jnp.broadcast_to(jnp.arange(N_GRP, dtype=jnp.int32)[:, None], (N_GRP, per_src))
    source_rows = hidden.reshape(N_GRP, per_src, FF)
    buckets = jnp.zeros((EXPERTS, N_GRP, CAP, FF), jnp.bfloat16)
    buckets = buckets.at[expert_ids, sources, slot_index].set(source_rows)

    def apply_expert(pair):
        pieces, weight = pair
        product = jnp.dot(pieces.reshape(N_GRP * CAP, FF).astype(jnp.float32), weight.astype(jnp.float32), precision=lax.Precision.HIGHEST)
        return product.astype(jnp.bfloat16).reshape(N_GRP, CAP, D)

    results = lax.map(apply_expert, (buckets, expert_weight))
    picked = results[expert_ids, sources, slot_index].reshape(TOKENS, TOPK, D).astype(jnp.float32)
    mixed = shared_out.astype(jnp.float32) + jnp.sum(gates[:, :, None] * picked, axis=1)
    return mixed.astype(jnp.bfloat16)
```

```python
import jax
import jax.numpy as jnp
from jax import lax
from jax.sharding import PartitionSpec as P

TOPG = 4
GROUP_DEV = 8


def bucketed(routes, gates, hidden, expert_weight, shared_out, experts, capacity):
    tokens_here = routes.shape[0]
    top_slots = routes.shape[1]
    hidden_width = hidden.shape[2]
    out_width = expert_weight.shape[2]
    expert_ids = routes.reshape(-1)
    onehot = (expert_ids[:, None] == jnp.arange(experts, dtype=jnp.int32)[None, :]).astype(
        jnp.int32
    )
    slot_index = jnp.sum((jnp.cumsum(onehot, axis=0) - onehot) * onehot, axis=1)
    flat_rows = hidden.reshape(-1, hidden_width)
    outgoing = (
        jnp.zeros((experts, capacity, hidden_width), jnp.bfloat16)
        .at[expert_ids, slot_index]
        .set(flat_rows)
    )
    weight = expert_weight[0]
    received = lax.all_to_all(outgoing, "grp", split_axis=0, concat_axis=0, tiled=True)
    leading = received.shape[0]
    count = received.shape[1]
    product = jnp.dot(
        received.reshape(leading * count, hidden_width), weight, preferred_element_type=jnp.float32
    )
    returned = lax.all_to_all(
        product.astype(jnp.bfloat16).reshape(leading, count, out_width),
        "grp",
        split_axis=0,
        concat_axis=0,
        tiled=True,
    )
    picked = returned[expert_ids, slot_index].reshape(tokens_here, top_slots, out_width)
    weighted = jnp.einsum("tk,tkd->td", gates, picked.astype(jnp.float32))
    mixed = shared_out.astype(jnp.float32) + weighted
    return mixed.astype(jnp.bfloat16)


def gated_blocks(routes, gates, hidden, experts):
    tokens, slots = routes.shape
    width = hidden.shape[2]
    ids = jnp.arange(experts, dtype=jnp.int32)
    match = routes[None] == ids[:, None, None]
    gate = jnp.sum(jnp.where(match, gates[None], 0.0), axis=2)
    owner = jnp.arange(tokens, dtype=jnp.int32)
    same = owner[:, None] == jnp.repeat(owner, slots)[None, :]
    pick = match.reshape(experts, 1, tokens * slots) & same[None]
    rows = jnp.dot(
        pick.reshape(experts * tokens, tokens * slots).astype(jnp.bfloat16),
        hidden.reshape(tokens * slots, width),
        preferred_element_type=jnp.float32,
    )
    rows = rows * gate.reshape(experts * tokens, 1)
    return rows.astype(jnp.bfloat16).reshape(experts, tokens, width)


def dense(routes, gates, hidden, expert_weight, shared_out, experts):
    tokens, width = routes.shape[0], hidden.shape[2]
    blocks = gated_blocks(routes, gates, hidden, experts)
    received = lax.all_to_all(blocks, "grp", split_axis=0, concat_axis=0, tiled=True)
    product = jnp.dot(
        received.reshape(experts * tokens, width),
        expert_weight[0],
        preferred_element_type=jnp.float32,
    )
    total = lax.psum_scatter(
        product.astype(jnp.bfloat16), "grp", scatter_dimension=0, tiled=True
    )
    return (shared_out.astype(jnp.float32) + total.astype(jnp.float32)).astype(jnp.bfloat16)


def per_device(routes, gates, hidden, expert_weight, shared_out):
    tokens_here = routes.shape[0]
    top_slots = routes.shape[1]
    experts = lax.axis_size("grp") * expert_weight.shape[0]
    groups = lax.axis_size("grp") // GROUP_DEV
    group_share = tokens_here * min(TOPG, groups) // groups
    capacity = min(group_share, max(2, 2 * tokens_here * top_slots // experts))
    if capacity == tokens_here:
        return dense(routes, gates, hidden, expert_weight, shared_out, experts)
    return bucketed(routes, gates, hidden, expert_weight, shared_out, experts, capacity)


def solution(mesh):
    in_specs = (
        P(("dom", "grp"), None),
        P(("dom", "grp"), None),
        P(("dom", "grp"), None, None),
        P("grp", None, None),
        P(("dom", "grp"), None),
    )
    out_specs = P(("dom", "grp"), None)
    return jax.shard_map(
        per_device, mesh=mesh, in_specs=in_specs, out_specs=out_specs, check_vma=False
    )
```

```python
import jax
import jax.numpy as jnp
from jax import lax
from jax.experimental import pallas as pl
from jax.experimental.pallas import tpu as pltpu
from jax.sharding import PartitionSpec as P

TOPG = 4
GROUP_DEV = 8


def bucketed(routes, gates, hidden, expert_weight, shared_out, experts, capacity):
    tokens_here = routes.shape[0]
    top_slots = routes.shape[1]
    hidden_width = hidden.shape[2]
    out_width = expert_weight.shape[2]
    expert_ids = routes.reshape(-1)
    onehot = (expert_ids[:, None] == jnp.arange(experts, dtype=jnp.int32)[None, :]).astype(
        jnp.int32
    )
    slot_index = jnp.sum((jnp.cumsum(onehot, axis=0) - onehot) * onehot, axis=1)
    flat_rows = hidden.reshape(-1, hidden_width)
    outgoing = (
        jnp.zeros((experts, capacity, hidden_width), jnp.bfloat16)
        .at[expert_ids, slot_index]
        .set(flat_rows)
    )
    weight = expert_weight[0]
    received = lax.all_to_all(outgoing, "grp", split_axis=0, concat_axis=0, tiled=True)
    leading = received.shape[0]
    count = received.shape[1]
    product = jnp.dot(
        received.reshape(leading * count, hidden_width), weight, preferred_element_type=jnp.float32
    )
    returned = lax.all_to_all(
        product.astype(jnp.bfloat16).reshape(leading, count, out_width),
        "grp",
        split_axis=0,
        concat_axis=0,
        tiled=True,
    )
    picked = returned[expert_ids, slot_index].reshape(tokens_here, top_slots, out_width)
    weighted = jnp.einsum("tk,tkd->td", gates, picked.astype(jnp.float32))
    mixed = shared_out.astype(jnp.float32) + weighted
    return mixed.astype(jnp.bfloat16)


def gated_blocks(routes, gates, hidden, experts):
    tokens, slots = routes.shape
    width = hidden.shape[2]
    ids = jnp.arange(experts, dtype=jnp.int32)
    match = routes[None] == ids[:, None, None]
    gate = jnp.sum(jnp.where(match, gates[None], 0.0), axis=2)
    owner = jnp.arange(tokens, dtype=jnp.int32)
    same = owner[:, None] == jnp.repeat(owner, slots)[None, :]
    pick = match.reshape(experts, 1, tokens * slots) & same[None]
    rows = jnp.dot(
        pick.reshape(experts * tokens, tokens * slots).astype(jnp.bfloat16),
        hidden.reshape(tokens * slots, width),
        preferred_element_type=jnp.float32,
    )
    rows = rows * gate.reshape(experts * tokens, 1)
    return rows.astype(jnp.bfloat16).reshape(experts, tokens, width)


CHUNKS = 7
ORDER = (0, 1, 3, 2)


def place(index):
    return index // 4, (index // 2) % 2, index % 2


def exchange_kernel(
    blocks_ref,
    w_hbm,
    shared_ref,
    out_ref,
    w_ref,
    rows,
    part,
    core_in,
    x_in,
    z_in,
    w_sem,
    own_sem,
    disp_send,
    disp_recv,
    core_send,
    core_recv,
    x_send,
    x_recv,
    z_send,
    z_recv,
):
    experts, tokens, width = blocks_ref.shape
    cw = out_ref.shape[1] // CHUNKS
    me = lax.axis_index("grp")
    z, x, c = place(me)
    partner = me + 1 - 2 * c
    across = me + 2 - 4 * x

    def far_z(s):
        if s == 0:
            return z
        if s == 1:
            return z + 1 - 2 * (z % 2)
        if s == 2:
            return (z + 2) % 4
        return 3 - z

    w_copy = pltpu.make_async_copy(w_hbm, w_ref, w_sem)
    w_copy.start()
    my_slot = c * 2 + x
    own_copy = pltpu.make_async_copy(blocks_ref.at[me], rows.at[z, my_slot], own_sem)
    own_copy.start()

    barrier = pltpu.get_barrier_semaphore()
    for i in range(1, experts):
        pl.semaphore_signal(
            barrier,
            inc=1,
            device_id={"grp": (me + i) % experts},
            device_id_type=pl.DeviceIdType.MESH,
        )
    pl.semaphore_wait(barrier, experts - 1)

    def dispatch_to(s, dx, dc):
        ox = 1 - x if dx else x
        oc = 1 - c if dc else c
        oz = far_z(s)
        other = oz * 4 + ox * 2 + oc
        sent = pltpu.make_async_remote_copy(
            src_ref=blocks_ref.at[other],
            dst_ref=rows.at[z, my_slot],
            send_sem=disp_send.at[s, dx * 2 + dc],
            recv_sem=disp_recv.at[s, dx * 2 + dc],
            device_id={"grp": other},
            device_id_type=pl.DeviceIdType.MESH,
        )
        came = pltpu.make_async_remote_copy(
            src_ref=blocks_ref.at[other],
            dst_ref=rows.at[oz, oc * 2 + ox],
            send_sem=disp_send.at[s, dx * 2 + dc],
            recv_sem=disp_recv.at[s, dx * 2 + dc],
            device_id={"grp": other},
            device_id_type=pl.DeviceIdType.MESH,
        )
        return sent, came

    def members(s):
        return [(dx, dc) for dx in (0, 1) for dc in (0, 1) if s or dx or dc]

    for dx, dc in members(0):
        dispatch_to(0, dx, dc)[0].start()
    for dx, dc in members(1):
        dispatch_to(1, dx, dc)[0].start()
        dispatch_to(3, dx, dc)[0].start()
    for dx, dc in members(2):
        dispatch_to(2, dx, dc)[0].start()

    def columns(j):
        return pl.ds(pl.multiple_of(j * cw, 128), cw)

    def core_copy(s, j):
        return pltpu.make_async_remote_copy(
            src_ref=part.at[s, j, 1 - c],
            dst_ref=core_in.at[s, j],
            send_sem=core_send.at[s, j],
            recv_sem=core_recv.at[s, j],
            device_id={"grp": partner},
            device_id_type=pl.DeviceIdType.MESH,
        )

    def x_copy(s, j):
        return pltpu.make_async_remote_copy(
            src_ref=part.at[s, j, c, 1 - x],
            dst_ref=x_in.at[s, j],
            send_sem=x_send.at[s, j],
            recv_sem=x_recv.at[s, j],
            device_id={"grp": across},
            device_id_type=pl.DeviceIdType.MESH,
        )

    def z_copy(s, j):
        goal = far_z(s)
        up = goal > z
        step = jnp.where(up, 1, -1)
        nxt = z + step
        slot = jnp.where(jnp.logical_and(nxt == goal, jnp.logical_not(up)), 4, goal)
        return pltpu.make_async_remote_copy(
            src_ref=part.at[s, j, c, x],
            dst_ref=z_in.at[slot, j],
            send_sem=z_send.at[s, j],
            recv_sem=z_recv.at[slot, j],
            device_id={"grp": me + 4 * step},
            device_id_type=pl.DeviceIdType.MESH,
        )

    def z_arrival(slot, j):
        return pltpu.make_async_remote_copy(
            src_ref=z_in.at[slot, j],
            dst_ref=z_in.at[slot, j],
            send_sem=z_send.at[1, j],
            recv_sem=z_recv.at[slot, j],
            device_id={"grp": partner},
            device_id_type=pl.DeviceIdType.MESH,
        )

    f32 = jnp.float32

    def multiply(s):
        for dx, dc in members(s):
            dispatch_to(s, dx, dc)[1].wait_recv()
        if s == 0:
            own_copy.wait()
            w_copy.wait()
        goal = far_z(s)

        @pl.loop(0, CHUNKS)
        def _(j):
            lhs = rows[goal].reshape(4 * tokens, width)
            res = jnp.dot(lhs, w_ref[:, columns(j)], preferred_element_type=f32)
            part[s, j] = res.astype(jnp.bfloat16).reshape(2, 2, tokens, cw)
            core_copy(s, j).start()

    def add_core(s):
        @pl.loop(0, CHUNKS)
        def _(j):
            core_copy(s, j).wait_recv()
            part[s, j, c, 1 - x] = (
                part[s, j, c, 1 - x].astype(f32) + core_in[s, j, 1 - x].astype(f32)
            ).astype(jnp.bfloat16)
            x_copy(s, j).start()
            part[s, j, c, x] = (
                part[s, j, c, x].astype(f32) + core_in[s, j, x].astype(f32)
            ).astype(jnp.bfloat16)

    def add_x(s, j):
        x_copy(s, j).wait_recv()
        part[s, j, c, x] = (
            part[s, j, c, x].astype(f32) + x_in[s, j].astype(f32)
        ).astype(jnp.bfloat16)

    def forward(s, j):
        z_arrival(far_z(s), j).wait_recv()
        part[s, j, c, x] = (
            part[s, j, c, x].astype(f32) + z_in[far_z(s), j].astype(f32)
        ).astype(jnp.bfloat16)
        z_copy(s, j).start()

    def handed(s):
        up = far_z(s) > z
        return jnp.logical_or(
            jnp.logical_and(up, z > 0), jnp.logical_and(jnp.logical_not(up), z < 3)
        )

    def stage_x(s):
        @pl.loop(0, CHUNKS)
        def _(j):
            add_x(s, j)
            if s:
                @pl.when(jnp.logical_not(handed(s)))
                def _():
                    z_copy(s, j).start()

    def stage_z(s):
        @pl.when(handed(s))
        def _():
            @pl.loop(0, CHUNKS)
            def _(j):
                forward(s, j)

    multiply(0)
    add_core(0)
    multiply(1)
    add_core(1)
    stage_x(0)
    multiply(3)
    add_core(3)
    stage_x(1)
    stage_x(3)
    multiply(2)
    add_core(2)

    @pl.loop(0, CHUNKS)
    def _(j):
        add_x(2, j)

        @pl.when(jnp.logical_not(handed(2)))
        def _():
            z_copy(2, j).start()

        @pl.when(handed(2))
        def _():
            forward(2, j)

    stage_z(3)
    stage_z(1)

    @pl.loop(0, CHUNKS)
    def _(j):
        @pl.when(z > 0)
        def _():
            z_arrival(z, j).wait_recv()

        @pl.when(z < 3)
        def _():
            z_arrival(4, j).wait_recv()

        total = shared_ref[:, columns(j)].astype(f32) + part[0, j, c, x].astype(f32)
        low = z_in[z, j].astype(f32)
        high = z_in[4, j].astype(f32)
        total = total + jnp.where(z > 0, low, 0.0) + jnp.where(z < 3, high, 0.0)
        out_ref[:, columns(j)] = total.astype(jnp.bfloat16)

    for s in ORDER:
        for dx, dc in members(s):
            dispatch_to(s, dx, dc)[0].wait_send()

        @pl.loop(0, CHUNKS)
        def _(j):
            core_copy(s, j).wait_send()
            x_copy(s, j).wait_send()
            if s:
                z_copy(s, j).wait_send()


def dense(routes, gates, hidden, expert_weight, shared_out, experts):
    tokens, width = routes.shape[0], hidden.shape[2]
    out_width = expert_weight.shape[2]
    cw = out_width // CHUNKS
    blocks = gated_blocks(routes, gates, hidden, experts)
    dma = pltpu.SemaphoreType.DMA
    vmem = pl.BlockSpec(memory_space=pltpu.VMEM)
    return pl.pallas_call(
        exchange_kernel,
        out_shape=jax.ShapeDtypeStruct((tokens, out_width), jnp.bfloat16),
        in_specs=[vmem, pl.BlockSpec(memory_space=pl.ANY), vmem],
        out_specs=vmem,
        scratch_shapes=[
            pltpu.VMEM((width, out_width), jnp.bfloat16),
            pltpu.VMEM((4, 4, tokens, width), jnp.bfloat16),
            pltpu.VMEM((4, CHUNKS, 2, 2, tokens, cw), jnp.bfloat16),
            pltpu.VMEM((4, CHUNKS, 2, tokens, cw), jnp.bfloat16),
            pltpu.VMEM((4, CHUNKS, tokens, cw), jnp.bfloat16),
            pltpu.VMEM((5, CHUNKS, tokens, cw), jnp.bfloat16),
            dma,
            dma,
            dma((4, 4)),
            dma((4, 4)),
            dma((4, CHUNKS)),
            dma((4, CHUNKS)),
            dma((4, CHUNKS)),
            dma((4, CHUNKS)),
            dma((4, CHUNKS)),
            dma((5, CHUNKS)),
        ],
        compiler_params=pltpu.CompilerParams(
            collective_id=0, has_side_effects=True, vmem_limit_bytes=48 * 1024 * 1024
        ),
        cost_estimate=pl.CostEstimate(
            flops=2 * experts * tokens * width * out_width,
            bytes_accessed=2 * width * out_width,
            transcendentals=0,
        ),
    )(blocks, expert_weight[0], shared_out)


def per_device(routes, gates, hidden, expert_weight, shared_out):
    tokens_here = routes.shape[0]
    top_slots = routes.shape[1]
    experts = lax.axis_size("grp") * expert_weight.shape[0]
    groups = lax.axis_size("grp") // GROUP_DEV
    group_share = tokens_here * min(TOPG, groups) // groups
    capacity = min(group_share, max(2, 2 * tokens_here * top_slots // experts))
    if capacity == tokens_here and experts == 16:
        return dense(routes, gates, hidden, expert_weight, shared_out, experts)
    return bucketed(routes, gates, hidden, expert_weight, shared_out, experts, capacity)


def solution(mesh):
    in_specs = (
        P(("dom", "grp"), None),
        P(("dom", "grp"), None),
        P(("dom", "grp"), None, None),
        P("grp", None, None),
        P(("dom", "grp"), None),
    )
    out_specs = P(("dom", "grp"), None)
    return jax.shard_map(
        per_device, mesh=mesh, in_specs=in_specs, out_specs=out_specs, check_vma=False
    )
```

```python
import jax
import jax.numpy as jnp
from jax import lax
from jax.experimental import pallas as pl
from jax.experimental.pallas import tpu as pltpu
from jax.sharding import PartitionSpec as P

TOPG = 4
GROUP_DEV = 8


def bucketed(routes, gates, hidden, expert_weight, shared_out, experts, capacity):
    tokens_here = routes.shape[0]
    top_slots = routes.shape[1]
    hidden_width = hidden.shape[2]
    out_width = expert_weight.shape[2]
    expert_ids = routes.reshape(-1)
    onehot = (expert_ids[:, None] == jnp.arange(experts, dtype=jnp.int32)[None, :]).astype(
        jnp.int32
    )
    slot_index = jnp.sum((jnp.cumsum(onehot, axis=0) - onehot) * onehot, axis=1)
    flat_rows = hidden.reshape(-1, hidden_width)
    outgoing = (
        jnp.zeros((experts, capacity, hidden_width), jnp.bfloat16)
        .at[expert_ids, slot_index]
        .set(flat_rows)
    )
    weight = expert_weight[0]
    received = lax.all_to_all(outgoing, "grp", split_axis=0, concat_axis=0, tiled=True)
    leading = received.shape[0]
    count = received.shape[1]
    product = jnp.dot(
        received.reshape(leading * count, hidden_width), weight, preferred_element_type=jnp.float32
    )
    returned = lax.all_to_all(
        product.astype(jnp.bfloat16).reshape(leading, count, out_width),
        "grp",
        split_axis=0,
        concat_axis=0,
        tiled=True,
    )
    picked = returned[expert_ids, slot_index].reshape(tokens_here, top_slots, out_width)
    weighted = jnp.einsum("tk,tkd->td", gates, picked.astype(jnp.float32))
    mixed = shared_out.astype(jnp.float32) + weighted
    return mixed.astype(jnp.bfloat16)


CHUNKS = 7
PHASES = (0, 1, 2, 3)


def place(index):
    return index // 4, (index // 2) % 2, index % 2


def exchange_kernel(
    routes_ref,
    gates_ref,
    hidden_ref,
    w_hbm,
    shared_ref,
    out_ref,
    w_ref,
    blocks_ref,
    rows,
    part,
    core_in,
    x_in,
    z_in,
    w_sem,
    disp_send,
    disp_recv,
    core_send,
    core_recv,
    x_send,
    x_recv,
    z_send,
    z_recv,
):
    experts, tokens, width = blocks_ref.shape
    slots = hidden_ref.shape[0] // tokens
    cw = out_ref.shape[1] // CHUNKS
    f32 = jnp.float32
    me = lax.axis_index("grp")
    z, x, c = place(me)
    partner = me + 1 - 2 * c
    across = me + 2 - 4 * x
    outer = jnp.logical_or(z == 0, z == 3)

    def far_z(s):
        if s == 0:
            return z
        if s == 1:
            return z + 1 - 2 * (z % 2)
        low = z < 2
        if s == 2:
            return jnp.where(low, 3, 0)
        return jnp.where(low, 2, 1)

    w_copy = pltpu.make_async_copy(w_hbm, w_ref, w_sem)
    w_copy.start()

    barrier = pltpu.get_barrier_semaphore()
    for i in range(1, experts):
        pl.semaphore_signal(
            barrier,
            inc=1,
            device_id={"grp": (me + i) % experts},
            device_id_type=pl.DeviceIdType.MESH,
        )

    def make_blocks(oz):
        shape = (tokens, tokens * slots)
        token = lax.broadcasted_iota(jnp.int32, shape, 0)
        same = token == lax.broadcasted_iota(jnp.int32, shape, 1) // slots
        picks, scales = [], []
        for i in range(4):
            pick = jnp.where(
                jnp.logical_and(same, routes_ref[...] == oz * 4 + i), 1.0, 0.0
            )
            scales.append(jnp.sum(pick * gates_ref[...], axis=1, keepdims=True))
            picks.append(pick.astype(jnp.bfloat16))
        made = jnp.dot(
            jnp.concatenate(picks, axis=0), hidden_ref[...], preferred_element_type=f32
        )
        made = made * jnp.concatenate(scales, axis=0)
        blocks_ref[pl.ds(oz * 4, 4)] = made.astype(jnp.bfloat16).reshape(4, tokens, width)

    my_slot = c * 2 + x

    def send_to(oz, dx, dc):
        ox = 1 - x if dx else x
        oc = 1 - c if dc else c
        other = oz * 4 + ox * 2 + oc
        return pltpu.make_async_remote_copy(
            src_ref=blocks_ref.at[other],
            dst_ref=rows.at[z, my_slot],
            send_sem=disp_send.at[oz, oc * 2 + ox],
            recv_sem=disp_recv.at[z, my_slot],
            device_id={"grp": other},
            device_id_type=pl.DeviceIdType.MESH,
        )

    def arrival(oz, dx, dc):
        ox = 1 - x if dx else x
        oc = 1 - c if dc else c
        return pltpu.make_async_remote_copy(
            src_ref=blocks_ref.at[me],
            dst_ref=rows.at[oz, oc * 2 + ox],
            send_sem=disp_send.at[oz, oc * 2 + ox],
            recv_sem=disp_recv.at[oz, oc * 2 + ox],
            device_id={"grp": oz * 4 + ox * 2 + oc},
            device_id_type=pl.DeviceIdType.MESH,
        )

    def members(s):
        return [(dx, dc) for dx in (0, 1) for dc in (0, 1) if s or dx or dc]

    near_z = far_z(1)
    across_z = (z + 2) % 4
    other_z = 3 - z

    def send_far():
        for dx, dc in members(1):
            send_to(other_z, dx, dc).start()
            send_to(across_z, dx, dc).start()

    make_blocks(z)
    pl.semaphore_wait(barrier, experts - 1)
    for dx, dc in members(0):
        send_to(z, dx, dc).start()
    rows[z, my_slot] = blocks_ref[me]
    make_blocks(near_z)
    for dx, dc in members(1):
        send_to(near_z, dx, dc).start()
    make_blocks(other_z)
    make_blocks(across_z)
    send_far()

    def columns(j):
        return pl.ds(pl.multiple_of(j * cw, 128), cw)

    def core_copy(s, j):
        return pltpu.make_async_remote_copy(
            src_ref=part.at[s, j, 1 - c],
            dst_ref=core_in.at[s, j],
            send_sem=core_send.at[s, j],
            recv_sem=core_recv.at[s, j],
            device_id={"grp": partner},
            device_id_type=pl.DeviceIdType.MESH,
        )

    def x_copy(s, j):
        return pltpu.make_async_remote_copy(
            src_ref=part.at[s, j, c, 1 - x],
            dst_ref=x_in.at[s, j],
            send_sem=x_send.at[s, j],
            recv_sem=x_recv.at[s, j],
            device_id={"grp": across},
            device_id_type=pl.DeviceIdType.MESH,
        )

    def z_copy(s, j):
        goal = far_z(s)
        up = goal > z
        step = jnp.where(up, 1, -1)
        nxt = z + step
        slot = jnp.where(jnp.logical_and(nxt == goal, jnp.logical_not(up)), 4, goal)
        return pltpu.make_async_remote_copy(
            src_ref=part.at[s, j, c, x],
            dst_ref=z_in.at[slot, j],
            send_sem=z_send.at[s, j],
            recv_sem=z_recv.at[slot, j],
            device_id={"grp": me + 4 * step},
            device_id_type=pl.DeviceIdType.MESH,
        )

    def z_arrival(slot, j):
        return pltpu.make_async_remote_copy(
            src_ref=z_in.at[slot, j],
            dst_ref=z_in.at[slot, j],
            send_sem=z_send.at[1, j],
            recv_sem=z_recv.at[slot, j],
            device_id={"grp": partner},
            device_id_type=pl.DeviceIdType.MESH,
        )

    def multiply(s):
        goal = far_z(s)
        for dx, dc in members(s):
            arrival(goal, dx, dc).wait_recv()
        if s == 0:
            w_copy.wait()

        @pl.loop(0, CHUNKS)
        def _(j):
            lhs = rows[goal].reshape(4 * tokens, width)
            res = jnp.dot(lhs, w_ref[:, columns(j)], preferred_element_type=f32)
            part[s, j] = res.astype(jnp.bfloat16).reshape(2, 2, tokens, cw)
            core_copy(s, j).start()

    def add_core(s):
        @pl.loop(0, CHUNKS)
        def _(j):
            core_copy(s, j).wait_recv()
            part[s, j, c, 1 - x] = (
                part[s, j, c, 1 - x].astype(f32) + core_in[s, j, 1 - x].astype(f32)
            ).astype(jnp.bfloat16)
            x_copy(s, j).start()
            part[s, j, c, x] = (
                part[s, j, c, x].astype(f32) + core_in[s, j, x].astype(f32)
            ).astype(jnp.bfloat16)

    def add_x(s, j):
        x_copy(s, j).wait_recv()
        part[s, j, c, x] = (
            part[s, j, c, x].astype(f32) + x_in[s, j].astype(f32)
        ).astype(jnp.bfloat16)

    def forward(s, j):
        z_arrival(far_z(s), j).wait_recv()
        part[s, j, c, x] = (
            part[s, j, c, x].astype(f32) + z_in[far_z(s), j].astype(f32)
        ).astype(jnp.bfloat16)
        z_copy(s, j).start()

    def handed(s):
        up = far_z(s) > z
        return jnp.logical_or(
            jnp.logical_and(up, z > 0), jnp.logical_and(jnp.logical_not(up), z < 3)
        )

    def stage_x(s):
        @pl.loop(0, CHUNKS)
        def _(j):
            add_x(s, j)
            if s:
                @pl.when(jnp.logical_not(handed(s)))
                def _():
                    z_copy(s, j).start()
            if s > 1:
                @pl.when(handed(s))
                def _():
                    forward(s, j)

    multiply(0)
    add_core(0)
    multiply(1)

    add_core(1)
    stage_x(0)
    multiply(2)
    add_core(2)
    stage_x(1)
    stage_x(2)
    multiply(3)
    add_core(3)

    @pl.when(handed(1))
    def _():
        @pl.loop(0, CHUNKS)
        def _(j):
            forward(1, j)

    stage_x(3)

    @pl.loop(0, CHUNKS)
    def _(j):
        @pl.when(z > 0)
        def _():
            z_arrival(z, j).wait_recv()

        @pl.when(z < 3)
        def _():
            z_arrival(4, j).wait_recv()

        total = shared_ref[:, columns(j)].astype(f32) + part[0, j, c, x].astype(f32)
        low = z_in[z, j].astype(f32)
        high = z_in[4, j].astype(f32)
        total = total + jnp.where(z > 0, low, 0.0) + jnp.where(z < 3, high, 0.0)
        out_ref[:, columns(j)] = total.astype(jnp.bfloat16)

    for s in PHASES:
        for dx, dc in members(s):
            send_to((z, near_z, across_z, other_z)[s], dx, dc).wait_send()

        @pl.loop(0, CHUNKS)
        def _(j):
            core_copy(s, j).wait_send()
            x_copy(s, j).wait_send()
            if s:
                z_copy(s, j).wait_send()


def dense(routes, gates, hidden, expert_weight, shared_out, experts):
    tokens, width = routes.shape[0], hidden.shape[2]
    out_width = expert_weight.shape[2]
    cw = out_width // CHUNKS
    slots = routes.shape[1]
    dma = pltpu.SemaphoreType.DMA
    vmem = pl.BlockSpec(memory_space=pltpu.VMEM)
    return pl.pallas_call(
        exchange_kernel,
        out_shape=jax.ShapeDtypeStruct((tokens, out_width), jnp.bfloat16),
        in_specs=[vmem, vmem, vmem, pl.BlockSpec(memory_space=pl.ANY), vmem],
        out_specs=vmem,
        scratch_shapes=[
            pltpu.VMEM((width, out_width), jnp.bfloat16),
            pltpu.VMEM((experts, tokens, width), jnp.bfloat16),
            pltpu.VMEM((4, 4, tokens, width), jnp.bfloat16),
            pltpu.VMEM((4, CHUNKS, 2, 2, tokens, cw), jnp.bfloat16),
            pltpu.VMEM((4, CHUNKS, 2, tokens, cw), jnp.bfloat16),
            pltpu.VMEM((4, CHUNKS, tokens, cw), jnp.bfloat16),
            pltpu.VMEM((5, CHUNKS, tokens, cw), jnp.bfloat16),
            dma,
            dma((4, 4)),
            dma((4, 4)),
            dma((4, CHUNKS)),
            dma((4, CHUNKS)),
            dma((4, CHUNKS)),
            dma((4, CHUNKS)),
            dma((4, CHUNKS)),
            dma((5, CHUNKS)),
        ],
        compiler_params=pltpu.CompilerParams(
            collective_id=0, has_side_effects=True, vmem_limit_bytes=48 * 1024 * 1024
        ),
        cost_estimate=pl.CostEstimate(
            flops=2 * experts * tokens * width * out_width,
            bytes_accessed=2 * width * out_width,
            transcendentals=0,
        ),
    )(
        routes.reshape(1, tokens * slots),
        gates.reshape(1, tokens * slots),
        hidden.reshape(tokens * slots, width),
        expert_weight[0],
        shared_out,
    )


def per_device(routes, gates, hidden, expert_weight, shared_out):
    tokens_here = routes.shape[0]
    top_slots = routes.shape[1]
    experts = lax.axis_size("grp") * expert_weight.shape[0]
    groups = lax.axis_size("grp") // GROUP_DEV
    group_share = tokens_here * min(TOPG, groups) // groups
    capacity = min(group_share, max(2, 2 * tokens_here * top_slots // experts))
    if capacity == tokens_here and experts == 16:
        return dense(routes, gates, hidden, expert_weight, shared_out, experts)
    return bucketed(routes, gates, hidden, expert_weight, shared_out, experts, capacity)


def solution(mesh):
    in_specs = (
        P(("dom", "grp"), None),
        P(("dom", "grp"), None),
        P(("dom", "grp"), None, None),
        P("grp", None, None),
        P(("dom", "grp"), None),
    )
    out_specs = P(("dom", "grp"), None)
    return jax.shard_map(
        per_device, mesh=mesh, in_specs=in_specs, out_specs=out_specs, check_vma=False
    )
```

```python
import jax
import jax.numpy as jnp
from jax import lax
from jax.experimental import pallas as pl
from jax.experimental.pallas import tpu as pltpu
from jax.sharding import PartitionSpec as P

TOPG = 4
GROUP_DEV = 8


def bucketed(routes, gates, hidden, expert_weight, shared_out, experts, capacity):
    tokens_here = routes.shape[0]
    top_slots = routes.shape[1]
    hidden_width = hidden.shape[2]
    out_width = expert_weight.shape[2]
    expert_ids = routes.reshape(-1)
    onehot = (expert_ids[:, None] == jnp.arange(experts, dtype=jnp.int32)[None, :]).astype(
        jnp.int32
    )
    slot_index = jnp.sum((jnp.cumsum(onehot, axis=0) - onehot) * onehot, axis=1)
    flat_rows = hidden.reshape(-1, hidden_width)
    outgoing = (
        jnp.zeros((experts, capacity, hidden_width), jnp.bfloat16)
        .at[expert_ids, slot_index]
        .set(flat_rows)
    )
    weight = expert_weight[0]
    received = lax.all_to_all(outgoing, "grp", split_axis=0, concat_axis=0, tiled=True)
    leading = received.shape[0]
    count = received.shape[1]
    product = jnp.dot(
        received.reshape(leading * count, hidden_width), weight, preferred_element_type=jnp.float32
    )
    returned = lax.all_to_all(
        product.astype(jnp.bfloat16).reshape(leading, count, out_width),
        "grp",
        split_axis=0,
        concat_axis=0,
        tiled=True,
    )
    picked = returned[expert_ids, slot_index].reshape(tokens_here, top_slots, out_width)
    weighted = jnp.einsum("tk,tkd->td", gates, picked.astype(jnp.float32))
    mixed = shared_out.astype(jnp.float32) + weighted
    return mixed.astype(jnp.bfloat16)


CHUNKS = 7
LAG = 2
PHASES = (0, 1, 2, 3)


def place(index):
    return index // 4, (index // 2) % 2, index % 2


def exchange_kernel(
    routes_ref,
    gates_ref,
    hidden_ref,
    w_hbm,
    shared_ref,
    out_ref,
    w_ref,
    blocks_ref,
    rows,
    part,
    core_in,
    x_in,
    z_in,
    w_sem,
    disp_send,
    disp_recv,
    core_send,
    core_recv,
    x_send,
    x_recv,
    z_send,
    z_recv,
):
    experts, tokens, width = blocks_ref.shape
    slots = hidden_ref.shape[0] // tokens
    cw = out_ref.shape[1] // CHUNKS
    f32 = jnp.float32
    me = lax.axis_index("grp")
    z, x, c = place(me)
    partner = me + 1 - 2 * c
    across = me + 2 - 4 * x
    outer = jnp.logical_or(z == 0, z == 3)

    def far_z(s):
        if s == 0:
            return z
        if s == 1:
            return z + 1 - 2 * (z % 2)
        low = z < 2
        if s == 2:
            return jnp.where(low, 3, 0)
        return jnp.where(low, 2, 1)

    w_copy = pltpu.make_async_copy(w_hbm, w_ref, w_sem)
    w_copy.start()

    barrier = pltpu.get_barrier_semaphore()
    for i in range(1, experts):
        pl.semaphore_signal(
            barrier,
            inc=1,
            device_id={"grp": (me + i) % experts},
            device_id_type=pl.DeviceIdType.MESH,
        )

    def make_blocks(oz):
        shape = (tokens, tokens * slots)
        token = lax.broadcasted_iota(jnp.int32, shape, 0)
        same = token == lax.broadcasted_iota(jnp.int32, shape, 1) // slots
        picks, scales = [], []
        for i in range(4):
            pick = jnp.where(
                jnp.logical_and(same, routes_ref[...] == oz * 4 + i), 1.0, 0.0
            )
            scales.append(jnp.sum(pick * gates_ref[...], axis=1, keepdims=True))
            picks.append(pick.astype(jnp.bfloat16))
        made = jnp.dot(
            jnp.concatenate(picks, axis=0), hidden_ref[...], preferred_element_type=f32
        )
        made = made * jnp.concatenate(scales, axis=0)
        blocks_ref[pl.ds(oz * 4, 4)] = made.astype(jnp.bfloat16).reshape(4, tokens, width)

    my_slot = c * 2 + x

    def send_to(oz, dx, dc):
        ox = 1 - x if dx else x
        oc = 1 - c if dc else c
        other = oz * 4 + ox * 2 + oc
        return pltpu.make_async_remote_copy(
            src_ref=blocks_ref.at[other],
            dst_ref=rows.at[z, my_slot],
            send_sem=disp_send.at[oz, oc * 2 + ox],
            recv_sem=disp_recv.at[z, my_slot],
            device_id={"grp": other},
            device_id_type=pl.DeviceIdType.MESH,
        )

    def arrival(oz, dx, dc):
        ox = 1 - x if dx else x
        oc = 1 - c if dc else c
        return pltpu.make_async_remote_copy(
            src_ref=blocks_ref.at[me],
            dst_ref=rows.at[oz, oc * 2 + ox],
            send_sem=disp_send.at[oz, oc * 2 + ox],
            recv_sem=disp_recv.at[oz, oc * 2 + ox],
            device_id={"grp": oz * 4 + ox * 2 + oc},
            device_id_type=pl.DeviceIdType.MESH,
        )

    def members(s):
        return [(dx, dc) for dx in (0, 1) for dc in (0, 1) if s or dx or dc]

    near_z = far_z(1)
    across_z = (z + 2) % 4
    other_z = 3 - z

    def send_far():
        for dx, dc in members(1):
            send_to(other_z, dx, dc).start()
            send_to(across_z, dx, dc).start()

    make_blocks(z)
    pl.semaphore_wait(barrier, experts - 1)
    for dx, dc in members(0):
        send_to(z, dx, dc).start()
    rows[z, my_slot] = blocks_ref[me]
    make_blocks(near_z)
    for dx, dc in members(1):
        send_to(near_z, dx, dc).start()
    make_blocks(other_z)
    make_blocks(across_z)
    send_far()

    def columns(j):
        return pl.ds(pl.multiple_of(j * cw, 128), cw)

    def core_copy(s, j):
        return pltpu.make_async_remote_copy(
            src_ref=part.at[s, j, 1 - c],
            dst_ref=core_in.at[s, j],
            send_sem=core_send.at[s, j],
            recv_sem=core_recv.at[s, j],
            device_id={"grp": partner},
            device_id_type=pl.DeviceIdType.MESH,
        )

    def x_copy(s, j):
        return pltpu.make_async_remote_copy(
            src_ref=part.at[s, j, c, 1 - x],
            dst_ref=x_in.at[s, j],
            send_sem=x_send.at[s, j],
            recv_sem=x_recv.at[s, j],
            device_id={"grp": across},
            device_id_type=pl.DeviceIdType.MESH,
        )

    def z_copy(s, j):
        goal = far_z(s)
        up = goal > z
        step = jnp.where(up, 1, -1)
        nxt = z + step
        slot = jnp.where(jnp.logical_and(nxt == goal, jnp.logical_not(up)), 4, goal)
        return pltpu.make_async_remote_copy(
            src_ref=part.at[s, j, c, x],
            dst_ref=z_in.at[slot, j],
            send_sem=z_send.at[s, j],
            recv_sem=z_recv.at[slot, j],
            device_id={"grp": me + 4 * step},
            device_id_type=pl.DeviceIdType.MESH,
        )

    def z_arrival(slot, j):
        return pltpu.make_async_remote_copy(
            src_ref=z_in.at[slot, j],
            dst_ref=z_in.at[slot, j],
            send_sem=z_send.at[1, j],
            recv_sem=z_recv.at[slot, j],
            device_id={"grp": partner},
            device_id_type=pl.DeviceIdType.MESH,
        )

    def add_core(s, j):
        core_copy(s, j).wait_recv()
        part[s, j, c, 1 - x] = (
            part[s, j, c, 1 - x].astype(f32) + core_in[s, j, 1 - x].astype(f32)
        ).astype(jnp.bfloat16)
        x_copy(s, j).start()
        part[s, j, c, x] = (
            part[s, j, c, x].astype(f32) + core_in[s, j, x].astype(f32)
        ).astype(jnp.bfloat16)

    def multiply(s):
        goal = far_z(s)
        for dx, dc in members(s):
            arrival(goal, dx, dc).wait_recv()
        if s == 0:
            w_copy.wait()

        @pl.loop(0, CHUNKS + LAG)
        def _(j):
            @pl.when(j < CHUNKS)
            def _():
                lhs = rows[goal].reshape(4 * tokens, width)
                res = jnp.dot(lhs, w_ref[:, columns(j)], preferred_element_type=f32)
                part[s, j] = res.astype(jnp.bfloat16).reshape(2, 2, tokens, cw)
                core_copy(s, j).start()

            @pl.when(j >= LAG)
            def _():
                add_core(s, j - LAG)

    def add_x(s, j):
        x_copy(s, j).wait_recv()
        part[s, j, c, x] = (
            part[s, j, c, x].astype(f32) + x_in[s, j].astype(f32)
        ).astype(jnp.bfloat16)

    def forward(s, j):
        z_arrival(far_z(s), j).wait_recv()
        part[s, j, c, x] = (
            part[s, j, c, x].astype(f32) + z_in[far_z(s), j].astype(f32)
        ).astype(jnp.bfloat16)
        z_copy(s, j).start()

    def handed(s):
        up = far_z(s) > z
        return jnp.logical_or(
            jnp.logical_and(up, z > 0), jnp.logical_and(jnp.logical_not(up), z < 3)
        )

    def stage_x(s):
        @pl.loop(0, CHUNKS)
        def _(j):
            add_x(s, j)
            if s:
                @pl.when(jnp.logical_not(handed(s)))
                def _():
                    z_copy(s, j).start()
            if s > 1:
                @pl.when(handed(s))
                def _():
                    forward(s, j)

    multiply(0)
    multiply(1)

    multiply(2)
    stage_x(1)
    multiply(3)
    stage_x(2)

    @pl.when(handed(1))
    def _():
        @pl.loop(0, CHUNKS)
        def _(j):
            forward(1, j)

    stage_x(3)
    stage_x(0)

    @pl.loop(0, CHUNKS)
    def _(j):
        @pl.when(z > 0)
        def _():
            z_arrival(z, j).wait_recv()

        @pl.when(z < 3)
        def _():
            z_arrival(4, j).wait_recv()

        total = shared_ref[:, columns(j)].astype(f32) + part[0, j, c, x].astype(f32)
        low = z_in[z, j].astype(f32)
        high = z_in[4, j].astype(f32)
        total = total + jnp.where(z > 0, low, 0.0) + jnp.where(z < 3, high, 0.0)
        out_ref[:, columns(j)] = total.astype(jnp.bfloat16)

    for s in PHASES:
        for dx, dc in members(s):
            send_to((z, near_z, across_z, other_z)[s], dx, dc).wait_send()

        @pl.loop(0, CHUNKS)
        def _(j):
            core_copy(s, j).wait_send()
            x_copy(s, j).wait_send()
            if s:
                z_copy(s, j).wait_send()


def dense(routes, gates, hidden, expert_weight, shared_out, experts):
    tokens, width = routes.shape[0], hidden.shape[2]
    out_width = expert_weight.shape[2]
    cw = out_width // CHUNKS
    slots = routes.shape[1]
    dma = pltpu.SemaphoreType.DMA
    vmem = pl.BlockSpec(memory_space=pltpu.VMEM)
    return pl.pallas_call(
        exchange_kernel,
        out_shape=jax.ShapeDtypeStruct((tokens, out_width), jnp.bfloat16),
        in_specs=[vmem, vmem, vmem, pl.BlockSpec(memory_space=pl.ANY), vmem],
        out_specs=vmem,
        scratch_shapes=[
            pltpu.VMEM((width, out_width), jnp.bfloat16),
            pltpu.VMEM((experts, tokens, width), jnp.bfloat16),
            pltpu.VMEM((4, 4, tokens, width), jnp.bfloat16),
            pltpu.VMEM((4, CHUNKS, 2, 2, tokens, cw), jnp.bfloat16),
            pltpu.VMEM((4, CHUNKS, 2, tokens, cw), jnp.bfloat16),
            pltpu.VMEM((4, CHUNKS, tokens, cw), jnp.bfloat16),
            pltpu.VMEM((5, CHUNKS, tokens, cw), jnp.bfloat16),
            dma,
            dma((4, 4)),
            dma((4, 4)),
            dma((4, CHUNKS)),
            dma((4, CHUNKS)),
            dma((4, CHUNKS)),
            dma((4, CHUNKS)),
            dma((4, CHUNKS)),
            dma((5, CHUNKS)),
        ],
        compiler_params=pltpu.CompilerParams(
            collective_id=0, has_side_effects=True, vmem_limit_bytes=48 * 1024 * 1024
        ),
        cost_estimate=pl.CostEstimate(
            flops=2 * experts * tokens * width * out_width,
            bytes_accessed=2 * width * out_width,
            transcendentals=0,
        ),
    )(
        routes.reshape(1, tokens * slots),
        gates.reshape(1, tokens * slots),
        hidden.reshape(tokens * slots, width),
        expert_weight[0],
        shared_out,
    )


def per_device(routes, gates, hidden, expert_weight, shared_out):
    tokens_here = routes.shape[0]
    top_slots = routes.shape[1]
    experts = lax.axis_size("grp") * expert_weight.shape[0]
    groups = lax.axis_size("grp") // GROUP_DEV
    group_share = tokens_here * min(TOPG, groups) // groups
    capacity = min(group_share, max(2, 2 * tokens_here * top_slots // experts))
    if capacity == tokens_here and experts == 16:
        return dense(routes, gates, hidden, expert_weight, shared_out, experts)
    return bucketed(routes, gates, hidden, expert_weight, shared_out, experts, capacity)


def solution(mesh):
    in_specs = (
        P(("dom", "grp"), None),
        P(("dom", "grp"), None),
        P(("dom", "grp"), None, None),
        P("grp", None, None),
        P(("dom", "grp"), None),
    )
    out_specs = P(("dom", "grp"), None)
    return jax.shard_map(
        per_device, mesh=mesh, in_specs=in_specs, out_specs=out_specs, check_vma=False
    )
```
